32 devices in a mesh: groups: 2 (over x), mp: 16 (over z, y, core).
Axes of the slice: x: 2, y: 2, z: 4, core: 2. Of those that a mesh axis runs over, the one named last changes fastest.
Arguments:
- activations: bfloat16 [128, 16384], P(('groups', 'mp')), parts along dimension 0, may hold values from -6 to 6
- gain: bfloat16 [16384], replicated, may hold values from 0.5 to 1.5
- q_weight: bfloat16 [16384, 16384], P(None, 'mp'), may hold values from -0.046875 to 0.046875
- kv_weight: bfloat16 [16384, 2048], P(None, 'mp'), may hold values from -0.046875 to 0.046875
- o_weight: bfloat16 [16384, 16384], P(None, 'mp'), may hold values from -0.75 to 0.75
- key_cache: bfloat16 [128, 8, 512, 128], P(('groups', 'mp')), parts along dimension 0, may hold values from -400 to 400
- value_cache: bfloat16 [128, 8, 512, 128], P(('groups', 'mp')), parts along dimension 0, may hold values from -6 to 6
- lengths: int32 [128], P(('groups', 'mp')), parts along dimension 0, may hold values from 1 to 512, as said below
Outputs:
- attention_out: bfloat16 [128, 16384], P('groups', 'mp'), parts along dimension 0
The draws below stay inside these ranges and needn't reach their ends.
There are 2 independent parts, one for each index of `groups`. The reference program is written for one: setup_inputs(seed, part) draws one part's arguments, and reference() takes and returns one part's arrays. A program takes and returns all parts, laid end to end along the dimension named above; an argument that names none is the same for every part. Nothing has to cross between parts.
Inputs may be any that keep to these rules, and one draw needn't show every extreme that they name: Request b attends to key_cache[b, :, t] and value_cache[b, :, t] for t < lengths[b]; some request has exactly 512.
All inputs are finite; a program needn't handle non-finite values.
Results may differ from the reference program's by a relative error of at most 0.007.
The reference program's roundings to bfloat16 on the way (of `normed` and `attended`) count: a program that leaves them out, or rounds other values in their place, can miss the bound.
Values may be sent and summed in bfloat16 or wider, within the bound.
No kernel may reach another device: no remote copies, remote signals or barrier semaphores. Data moves between devices by JAX's collectives and lax.ppermute only.
A program may use at most 128 MiB of HBM per device.

```python
import math
import jax
import jax.numpy as jnp
from jax import lax

D = 16384
HEADS = 128
KV_HEADS = 8
HEAD_DIM = 128
CACHE = 512
BATCH = 64


def draw_key_cache(key, part):
    shape = (BATCH, KV_HEADS, CACHE, HEAD_DIM)
    base = jax.random.normal(jax.random.fold_in(key, 11), shape, jnp.float32)
    return jnp.clip(base, -400.0, 400.0).astype(jnp.bfloat16)


def draw_lengths(key, part):
    drawn = jax.random.randint(jax.random.fold_in(key, 21), (BATCH,), 1, CACHE + 1, dtype=jnp.int32)
    chosen = jax.random.randint(jax.random.fold_in(key, 22), (), 0, BATCH, dtype=jnp.int32)
    return jnp.where(jnp.arange(BATCH, dtype=jnp.int32) == chosen, CACHE, drawn).astype(jnp.int32)


def levels(rng, shape, pieces, smallest, largest):
    factor_of = 1.0
    for axis_at, shards_of in pieces:
        draws = jax.random.uniform(jax.random.fold_in(jax.random.fold_in(rng, 6), axis_at), (shards_of,), jnp.float32, smallest / len(pieces), largest / len(pieces))
        factor_of = factor_of * jnp.repeat(jnp.exp(draws), shape[axis_at] // shards_of).reshape((-1,) + (1,) * (len(shape) - 1 - axis_at))
    return factor_of


def scatter_about(key, dims, scale, reach, split=(), kind=jnp.bfloat16):
    factor_of = levels(key, dims, split, -0.22, 0.18) if split else 1.0
    result = jax.random.normal(key, dims, jnp.float32) * scale * factor_of
    return jnp.minimum(jnp.maximum(result, -reach), reach).astype(kind)


def setup_inputs(seed: int = 0, part: int = 0) -> dict:
    streams_of = jax.random.split(jax.random.key(seed), 9)
    own_keys = jax.random.split(jax.random.fold_in(streams_of[8], part), 9)
    return {
        "activations": scatter_about(own_keys[0], (BATCH, D), 1.0, 6.0, ((0, 16),)),
        "gain": jnp.clip(1.0 + 0.1 * jax.random.normal(streams_of[1], (D,), jnp.float32), 0.5, 1.5).astype(jnp.bfloat16),
        "q_weight": scatter_about(streams_of[2], (D, HEADS * HEAD_DIM), D ** -0.5, 0.046875, ((1, 16),)),
        "kv_weight": scatter_about(streams_of[3], (D, 2 * KV_HEADS * HEAD_DIM), D ** -0.5, 0.046875, ((1, 16),)),
        "o_weight": scatter_about(streams_of[4], (HEADS * HEAD_DIM, D), 0.125, 0.75, ((1, 16),)),
        "key_cache": draw_key_cache(jax.random.fold_in(jax.random.fold_in(streams_of[8], part), 71), part),
        "value_cache": scatter_about(own_keys[6], (BATCH, KV_HEADS, CACHE, HEAD_DIM), 1.0, 6.0, ((0, 16),)),
        "lengths": draw_lengths(jax.random.fold_in(jax.random.fold_in(streams_of[8], part), 71), part),
    }


rope_base = 500000.0
norm_eps = 1e-05

def rotate(vector, position):
    middle = vector.shape[-1] // 2
    offsets = jnp.arange(middle, dtype=jnp.float32)
    frequency = jnp.exp(offsets * (-2.0 * math.log(rope_base) / vector.shape[-1]))
    angles = position * frequency
    cosine = jnp.cos(angles)
    sine = jnp.sin(angles)
    leading = vector[..., :middle]
    trailing = vector[..., middle:]
    return jnp.concatenate([leading * cosine - trailing * sine, trailing * cosine + leading * sine], axis=-1)

def normalize(activations, gain):
    widened = activations.astype(jnp.float32)
    inverse = lax.rsqrt(lax.optimization_barrier(jnp.mean(widened * widened, axis=-1, keepdims=True)) + norm_eps)
    return (widened * inverse * gain.astype(jnp.float32)).astype(jnp.bfloat16)

def one_request(items):
    query_row, pair_row, key_rows, value_rows, length = items
    per_group = HEADS // KV_HEADS
    position = length.astype(jnp.float32)
    scaling = 1.0 / math.sqrt(HEAD_DIM)
    query = rotate(query_row.astype(jnp.float32).reshape(KV_HEADS, per_group, HEAD_DIM), position).astype(jnp.bfloat16)
    fresh_key = rotate(pair_row[:KV_HEADS * HEAD_DIM].astype(jnp.float32).reshape(KV_HEADS, HEAD_DIM), position).astype(jnp.bfloat16)
    fresh_value = pair_row[KV_HEADS * HEAD_DIM:].reshape(KV_HEADS, HEAD_DIM)
    scores = jnp.einsum('gqd,gtd->gqt', query.astype(jnp.float32), key_rows.astype(jnp.float32)) * scaling
    visible = jnp.arange(CACHE, dtype=jnp.int32) < length
    scores = jnp.where(visible[None, None, :], scores, -1e+30)
    own = jnp.einsum('gqd,gd->gq', query.astype(jnp.float32), fresh_key.astype(jnp.float32)) * scaling
    highest = jnp.maximum(lax.optimization_barrier(jnp.max(scores, axis=-1)), own)
    weights = jnp.where(visible[None, None, :], jnp.exp(scores - highest[..., None]), 0.0)
    own_weight = jnp.exp(own - highest)
    denominator = lax.optimization_barrier(jnp.sum(weights, axis=-1)) + own_weight
    probs = (weights / denominator[..., None]).astype(jnp.bfloat16)
    own_prob = (own_weight / denominator).astype(jnp.bfloat16)
    mixed = jnp.einsum('gqt,gtd->gqd', probs.astype(jnp.float32), value_rows.astype(jnp.float32))
    mixed = mixed + own_prob.astype(jnp.float32)[..., None] * fresh_value.astype(jnp.float32)[:, None, :]
    return mixed.reshape(HEADS * HEAD_DIM).astype(jnp.bfloat16)

def reference(activations, gain, q_weight, kv_weight, o_weight, key_cache, value_cache, lengths):
    normed = normalize(activations, gain)
    query = jnp.dot(normed, q_weight, preferred_element_type=jnp.float32).astype(jnp.bfloat16)
    pairs = jnp.dot(normed, kv_weight, preferred_element_type=jnp.float32).astype(jnp.bfloat16)
    attended = lax.map(one_request, (query, pairs, key_cache, value_cache, lengths))
    return jnp.dot(attended, o_weight, preferred_element_type=jnp.float32).astype(jnp.bfloat16)
```

```python
import math

import jax
import jax.numpy as jnp
from jax import lax
from jax.sharding import PartitionSpec as P

HEADS = 128
KV_HEADS = 8
HEAD_DIM = 128
CACHE = 512


rope_base = 500000.0
norm_eps = 1e-05


def rotate(vector, position):
    middle = vector.shape[-1] // 2
    offsets = jnp.arange(middle, dtype=jnp.float32)
    frequency = jnp.exp(offsets * (-2.0 * math.log(rope_base) / vector.shape[-1]))
    angles = position * frequency
    cosine = jnp.cos(angles)
    sine = jnp.sin(angles)
    leading = vector[..., :middle]
    trailing = vector[..., middle:]
    return jnp.concatenate(
        [leading * cosine - trailing * sine, trailing * cosine + leading * sine], axis=-1
    )


def normalize(activations, gain):
    widened = activations.astype(jnp.float32)
    inverse = lax.rsqrt(jnp.mean(widened * widened, axis=-1, keepdims=True) + norm_eps)
    return (widened * inverse * gain.astype(jnp.float32)).astype(jnp.bfloat16)


def swap(block, size, distance):
    return lax.ppermute(block, "mp", [(i, i ^ distance) for i in range(size)])


def gather_blocks(block, size):
    held = {0: block}
    for far in (8, 4, 12):
        if far < size:
            held[far] = swap(block, size, far)
    held[2] = swap(block, size, 2)
    for far in (4, 8, 12):
        if far < size:
            held[far ^ 2] = swap(held[far], size, 2)
    for even in range(0, size, 2):
        held[even ^ 1] = swap(held[even], size, 1)
    return [held[r] for r in range(size)]


def gather_rows(block, size):
    rows = block.shape[0]
    if size not in (4, 8, 16):
        gathered = lax.all_gather(block, "mp", axis=0, tiled=True)
        return gathered, None
    gathered = jnp.concatenate(gather_blocks(block, size), axis=0)
    me = lax.axis_index("mp")
    to = jnp.arange(size * rows, dtype=jnp.int32)[:, None]
    source = jnp.arange(size * rows, dtype=jnp.int32)[None, :]
    place = (to == ((source // rows) ^ me) * rows + source % rows).astype(block.dtype)
    return gathered, place


def in_order(place, values):
    if place is None:
        return values
    return jnp.dot(place, values, preferred_element_type=jnp.float32).astype(values.dtype)


def shards(activations, gain, q_weight, kv_weight, o_weight, key_cache, value_cache, lengths):
    normed = normalize(activations, gain)
    size = lax.axis_size("mp")
    piece, place = gather_rows(normed, size)
    projected = jnp.concatenate(
        [
            jnp.dot(piece, q_weight, preferred_element_type=jnp.float32),
            jnp.dot(piece, kv_weight, preferred_element_type=jnp.float32),
        ],
        axis=1,
    ).astype(jnp.bfloat16)
    projected = in_order(place, projected)
    query_cols = q_weight.shape[1]
    query_all, pairs_all = (
        lax.all_to_all(projected[:, :query_cols], "mp", split_axis=0, concat_axis=1, tiled=True),
        lax.all_to_all(projected[:, query_cols:], "mp", split_axis=0, concat_axis=1, tiled=True),
    )
    requests = query_all.shape[0]
    per_group = HEADS // KV_HEADS
    scaling = 1.0 / math.sqrt(HEAD_DIM)
    position = lengths.astype(jnp.float32)
    query = rotate(
        query_all.astype(jnp.float32).reshape(requests, KV_HEADS, per_group, HEAD_DIM),
        position[:, None, None, None],
    ).astype(jnp.bfloat16)
    fresh_key = rotate(
        pairs_all[:, : KV_HEADS * HEAD_DIM]
        .astype(jnp.float32)
        .reshape(requests, KV_HEADS, HEAD_DIM),
        position[:, None, None],
    ).astype(jnp.bfloat16)
    fresh_value = pairs_all[:, KV_HEADS * HEAD_DIM :].reshape(requests, KV_HEADS, HEAD_DIM)
    scores = (
        jnp.einsum("rgqd,rgtd->rgqt", query, key_cache, preferred_element_type=jnp.float32)
        * scaling
    )
    visible = jnp.arange(CACHE, dtype=jnp.int32)[None, :] < lengths[:, None]
    scores = jnp.where(visible[:, None, None, :], scores, -1e30)
    own = (
        jnp.einsum("rgqd,rgd->rgq", query, fresh_key, preferred_element_type=jnp.float32) * scaling
    )
    highest = jnp.maximum(jnp.max(scores, axis=-1), own)
    weights = jnp.where(visible[:, None, None, :], jnp.exp(scores - highest[..., None]), 0.0)
    own_weight = jnp.exp(own - highest)
    denominator = jnp.sum(weights, axis=-1) + own_weight
    probs = (weights / denominator[..., None]).astype(jnp.bfloat16)
    own_prob = (own_weight / denominator).astype(jnp.bfloat16)
    mixed = jnp.einsum("rgqt,rgtd->rgqd", probs, value_cache, preferred_element_type=jnp.float32)
    mixed = (
        mixed
        + own_prob.astype(jnp.float32)[..., None] * fresh_value.astype(jnp.float32)[:, :, None, :]
    )
    attended = mixed.reshape(requests, HEADS * HEAD_DIM).astype(jnp.bfloat16)
    everyone, place = gather_rows(attended, size)
    result = jnp.dot(everyone, o_weight, preferred_element_type=jnp.float32)
    return in_order(place, result.astype(jnp.bfloat16))


def solution(mesh):
    placed = (
        P(("groups", "mp"), None),
        P(),
        P(None, "mp"),
        P(None, "mp"),
        P(None, "mp"),
        P(("groups", "mp"), None, None, None),
        P(("groups", "mp"), None, None, None),
        P(("groups", "mp")),
    )
    return jax.shard_map(
        shards, mesh=mesh, in_specs=placed, out_specs=P("groups", "mp"), check_vma=False
    )
```

```python
import functools
import math

import jax
import jax.numpy as jnp
from jax import lax
from jax.experimental import pallas as pl
from jax.experimental.pallas import tpu as pltpu
from jax.sharding import PartitionSpec as P

HEADS = 128
KV_HEADS = 8
HEAD_DIM = 128
CACHE = 512

MIB = 1 << 20
STEP = 2048
LANES = 128

rope_base = 500000.0
norm_eps = 1e-05

IN_VMEM = pl.BlockSpec(memory_space=pltpu.VMEM)
IN_HBM = pl.BlockSpec(memory_space=pltpu.HBM)
IN_SMEM = pl.BlockSpec(memory_space=pltpu.SMEM)


def rotate(vector, position):
    middle = vector.shape[-1] // 2
    offsets = jnp.arange(middle, dtype=jnp.float32)
    frequency = jnp.exp(offsets * (-2.0 * math.log(rope_base) / vector.shape[-1]))
    angles = position * frequency
    cosine = jnp.cos(angles)
    sine = jnp.sin(angles)
    leading = vector[..., :middle]
    trailing = vector[..., middle:]
    return jnp.concatenate(
        [leading * cosine - trailing * sine, trailing * cosine + leading * sine], axis=-1
    )


def norm_kernel(x_hbm, gain_hbm, out_ref, x_ref, gain_ref, sems):
    copies = [
        pltpu.make_async_copy(x_hbm, x_ref, sems.at[0]),
        pltpu.make_async_copy(gain_hbm, gain_ref, sems.at[1]),
    ]
    for copy in copies:
        copy.start()
    for copy in copies:
        copy.wait()
    widened = x_ref[...].astype(jnp.float32)
    inverse = lax.rsqrt(jnp.mean(widened * widened, axis=-1, keepdims=True) + norm_eps)
    lanes = gain_ref.shape[1]
    for j in range(gain_ref.shape[0]):
        columns = pl.ds(j * lanes, lanes)
        gain = gain_ref[pl.ds(j, 1), :].astype(jnp.float32)
        out_ref[:, columns] = (x_ref[:, columns].astype(jnp.float32) * inverse * gain).astype(
            out_ref.dtype
        )


def normalize(activations, gain):
    return pl.pallas_call(
        norm_kernel,
        out_shape=pltpu.VMEM(activations.shape, jnp.bfloat16),
        in_specs=[IN_HBM, IN_HBM],
        out_specs=IN_VMEM,
        scratch_shapes=[
            pltpu.VMEM(activations.shape, activations.dtype),
            pltpu.VMEM((gain.shape[0] // LANES, LANES), gain.dtype),
            pltpu.SemaphoreType.DMA((2,)),
        ],
        compiler_params=pltpu.CompilerParams(vmem_limit_bytes=56 * MIB),
        name="norm",
    )(activations, gain.reshape(-1, LANES))


def swap(block, size, distance):
    return lax.ppermute(block, "mp", [(i, i ^ distance) for i in range(size)])


def gather_blocks(block, size):
    held = {0: block}
    for far in (8, 4, 12):
        if far < size:
            held[far] = swap(block, size, far)
    held[2] = swap(block, size, 2)
    for far in (4, 8, 12):
        if far < size:
            held[far ^ 2] = swap(held[far], size, 2)
    for even in range(0, size, 2):
        held[even ^ 1] = swap(held[even], size, 1)
    return [held[r] for r in range(size)]


def load_kernel(parts, w_ref, out_ref, sems):
    rows = out_ref.shape[0] // parts
    copies = [
        pltpu.make_async_copy(
            w_ref.at[pl.ds(i * rows, rows)], out_ref.at[pl.ds(i * rows, rows)], sems.at[i]
        )
        for i in range(parts)
    ]
    for copy in copies:
        copy.start()
    for copy in copies:
        copy.wait()


def load(weight, rows):
    parts = 4
    return pl.pallas_call(
        functools.partial(load_kernel, parts),
        out_shape=pltpu.VMEM((rows, weight.shape[1]), weight.dtype),
        in_specs=[IN_HBM],
        out_specs=IN_VMEM,
        scratch_shapes=[pltpu.SemaphoreType.DMA((parts,))],
        cost_estimate=pl.CostEstimate(
            flops=0, bytes_accessed=rows * weight.shape[1] * 2, transcendentals=0
        ),
        compiler_params=pltpu.CompilerParams(vmem_limit_bytes=36 * MIB),
        name="load",
    )(weight)


def product_kernel(count, streamed, ordered, *refs):
    me_ref, blocks, resident = refs[0], refs[1 : 1 + count], refs[1 + count]
    weights = refs[2 + count : 2 + count + streamed]
    out_ref = refs[2 + count + streamed]
    buffers = refs[3 + count + streamed : 3 + count + 2 * streamed]
    total, sems = refs[3 + count + 2 * streamed :]
    depth = blocks[0].shape[1]
    rows = blocks[0].shape[0]
    held = resident.shape[0]
    main = resident.shape[1]
    copies = {}
    for w, (weight, buffer) in enumerate(zip(weights, buffers)):
        first = held if w == 0 else 0
        for at in range(first, depth, STEP):
            copies[w, at] = pltpu.make_async_copy(
                weight.at[pl.ds(at, STEP)],
                buffer.at[pl.ds(at - first, STEP)],
                sems.at[w, at // STEP],
            )
    for key in sorted(copies, key=lambda k: (k[1], k[0])):
        copies[key].start()

    def joined(at):
        return jnp.concatenate([block[:, pl.ds(at, STEP)] for block in blocks], axis=0)

    for at in range(0, depth, STEP):
        x = joined(at)
        column = 0
        for w, (weight, buffer) in enumerate(zip(weights, buffers)):
            if (w, at) in copies:
                copies[w, at].wait()
                piece = buffer[pl.ds(at - (held if w == 0 else 0), STEP), :]
            else:
                piece = resident[pl.ds(at, STEP), :]
            columns = pl.ds(column, weight.shape[1])
            term = jnp.dot(x, piece, preferred_element_type=jnp.float32)
            if at == 0:
                total[:, columns] = term
            else:
                total[:, columns] += term
            column += weight.shape[1]
    me = me_ref[0]
    if ordered:
        to = lax.broadcasted_iota(jnp.int32, (count * rows, count * rows), 0)
        source = lax.broadcasted_iota(jnp.int32, (count * rows, count * rows), 1)
        place = to == ((source // rows) ^ me) * rows + source % rows
        out_ref[...] = jnp.dot(
            place.astype(jnp.bfloat16),
            total[...].astype(jnp.bfloat16),
            preferred_element_type=jnp.float32,
        ).astype(out_ref.dtype)
    else:
        for r in range(count):
            out_ref[me ^ r] = total[pl.ds(r * rows, rows), :].astype(out_ref.dtype)


def product(me, blocks, resident, weights, ordered):
    count, (rows, depth) = len(blocks), blocks[0].shape
    columns = sum(w.shape[1] for w in weights)
    held = resident.shape[0]
    shape = (count * rows, columns) if ordered else (count, rows, columns)
    spaces = [
        pltpu.VMEM((depth - (held if i == 0 else 0), w.shape[1]), w.dtype)
        for i, w in enumerate(weights)
    ]
    pinned = [pltpu.with_memory_space_constraint(b, pltpu.VMEM) for b in blocks]
    streamed_bytes = sum(2 * s.shape[0] * s.shape[1] for s in spaces)
    return pl.pallas_call(
        functools.partial(product_kernel, count, len(weights), ordered),
        out_shape=jax.ShapeDtypeStruct(shape, jnp.bfloat16),
        in_specs=[IN_SMEM] + [IN_VMEM] * (count + 1) + [IN_HBM] * len(weights),
        out_specs=IN_VMEM,
        scratch_shapes=[
            *spaces,
            pltpu.VMEM((count * rows, columns), jnp.float32),
            pltpu.SemaphoreType.DMA((len(weights), depth // STEP)),
        ],
        cost_estimate=pl.CostEstimate(
            flops=2 * count * rows * depth * columns,
            bytes_accessed=streamed_bytes,
            transcendentals=0,
        ),
        compiler_params=pltpu.CompilerParams(vmem_limit_bytes=44 * MIB),
        name="product",
    )(me, *pinned, pltpu.with_memory_space_constraint(resident, pltpu.VMEM), *weights)


def attend(query_all, pairs_all, key_cache, value_cache, lengths):
    requests = query_all.shape[0]
    per_group = HEADS // KV_HEADS
    scaling = 1.0 / math.sqrt(HEAD_DIM)
    position = lengths.astype(jnp.float32)
    query = rotate(
        query_all.astype(jnp.float32).reshape(requests, KV_HEADS, per_group, HEAD_DIM),
        position[:, None, None, None],
    ).astype(jnp.bfloat16)
    fresh_key = rotate(
        pairs_all[:, : KV_HEADS * HEAD_DIM]
        .astype(jnp.float32)
        .reshape(requests, KV_HEADS, HEAD_DIM),
        position[:, None, None],
    ).astype(jnp.bfloat16)
    fresh_value = pairs_all[:, KV_HEADS * HEAD_DIM :].reshape(requests, KV_HEADS, HEAD_DIM)
    scores = (
        jnp.einsum("rgqd,rgtd->rgqt", query, key_cache, preferred_element_type=jnp.float32)
        * scaling
    )
    visible = jnp.arange(CACHE, dtype=jnp.int32)[None, :] < lengths[:, None]
    scores = jnp.where(visible[:, None, None, :], scores, -1e30)
    own = (
        jnp.einsum("rgqd,rgd->rgq", query, fresh_key, preferred_element_type=jnp.float32) * scaling
    )
    highest = jnp.maximum(jnp.max(scores, axis=-1), own)
    weights = jnp.where(visible[:, None, None, :], jnp.exp(scores - highest[..., None]), 0.0)
    own_weight = jnp.exp(own - highest)
    denominator = jnp.sum(weights, axis=-1) + own_weight
    probs = (weights / denominator[..., None]).astype(jnp.bfloat16)
    own_prob = (own_weight / denominator).astype(jnp.bfloat16)
    mixed = jnp.einsum("rgqt,rgtd->rgqd", probs, value_cache, preferred_element_type=jnp.float32)
    mixed = (
        mixed
        + own_prob.astype(jnp.float32)[..., None] * fresh_value.astype(jnp.float32)[:, :, None, :]
    )
    return mixed.reshape(requests, HEADS * HEAD_DIM).astype(jnp.bfloat16)


def shards(activations, gain, q_weight, kv_weight, o_weight, key_cache, value_cache, lengths):
    size = lax.axis_size("mp")
    normed = normalize(activations, gain)
    query_cols = q_weight.shape[1]
    by_swaps = size in (4, 8, 16)
    me = lax.axis_index("mp").astype(jnp.int32).reshape(1)
    if by_swaps:
        held = q_weight.shape[0] * 3 // 8 // STEP * STEP
        projected = product(
            me, gather_blocks(normed, size), load(q_weight, held), [q_weight, kv_weight], False
        )
    else:
        piece = lax.all_gather(normed, "mp", axis=0, tiled=True)
        projected = jnp.concatenate(
            [
                jnp.dot(piece, q_weight, preferred_element_type=jnp.float32),
                jnp.dot(piece, kv_weight, preferred_element_type=jnp.float32),
            ],
            axis=1,
        ).astype(jnp.bfloat16).reshape(size, normed.shape[0], -1)
    arrived = lax.all_to_all(projected, "mp", split_axis=0, concat_axis=0, tiled=True)
    arrived = arrived.transpose(1, 0, 2)
    requests = arrived.shape[0]
    attended = attend(
        arrived[..., :query_cols].reshape(requests, -1),
        arrived[..., query_cols:].reshape(requests, -1),
        key_cache,
        value_cache,
        lengths,
    )
    if by_swaps:
        held = o_weight.shape[0] * 3 // 8 // STEP * STEP
        return product(me, gather_blocks(attended, size), load(o_weight, held), [o_weight], True)
    everyone = lax.all_gather(attended, "mp", axis=0, tiled=True)
    return jnp.dot(everyone, o_weight, preferred_element_type=jnp.float32).astype(jnp.bfloat16)


def solution(mesh):
    placed = (
        P(("groups", "mp"), None),
        P(),
        P(None, "mp"),
        P(None, "mp"),
        P(None, "mp"),
        P(("groups", "mp"), None, None, None),
        P(("groups", "mp"), None, None, None),
        P(("groups", "mp")),
    )
    return jax.shard_map(
        shards, mesh=mesh, in_specs=placed, out_specs=P("groups", "mp"), check_vma=False
    )
```

```python
import functools
import math

import jax
import jax.numpy as jnp
from jax import lax
from jax.experimental import pallas as pl
from jax.experimental.pallas import tpu as pltpu
from jax.sharding import PartitionSpec as P

HEADS = 128
KV_HEADS = 8
HEAD_DIM = 128
CACHE = 512

MIB = 1 << 20
STEP = 2048
LANES = 128
QUERY_LOADED = 4
OUT_LOADED = 5
PRODUCT_MIB = 30

rope_base = 500000.0
norm_eps = 1e-05

IN_VMEM = pl.BlockSpec(memory_space=pltpu.VMEM)
IN_HBM = pl.BlockSpec(memory_space=pltpu.HBM)
IN_SMEM = pl.BlockSpec(memory_space=pltpu.SMEM)


def rotate(vector, position):
    middle = vector.shape[-1] // 2
    offsets = jnp.arange(middle, dtype=jnp.float32)
    frequency = jnp.exp(offsets * (-2.0 * math.log(rope_base) / vector.shape[-1]))
    angles = position * frequency
    cosine = jnp.cos(angles)
    sine = jnp.sin(angles)
    leading = vector[..., :middle]
    trailing = vector[..., middle:]
    return jnp.concatenate(
        [leading * cosine - trailing * sine, trailing * cosine + leading * sine], axis=-1
    )


def near(array):
    return pltpu.with_memory_space_constraint(array, pltpu.VMEM)


def far(array):
    return pltpu.with_memory_space_constraint(array, pltpu.HBM)


def norm_kernel(x_hbm, gain_hbm, out_ref, x_ref, gain_ref, sems):
    copies = [
        pltpu.make_async_copy(x_hbm, x_ref, sems.at[0]),
        pltpu.make_async_copy(gain_hbm, gain_ref, sems.at[1]),
    ]
    for copy in copies:
        copy.start()
    for copy in copies:
        copy.wait()
    widened = x_ref[...].astype(jnp.float32)
    inverse = lax.rsqrt(jnp.mean(widened * widened, axis=-1, keepdims=True) + norm_eps)
    lanes = gain_ref.shape[1]
    for j in range(gain_ref.shape[0]):
        columns = pl.ds(j * lanes, lanes)
        gain = gain_ref[pl.ds(j, 1), :].astype(jnp.float32)
        out_ref[:, columns] = (x_ref[:, columns].astype(jnp.float32) * inverse * gain).astype(
            out_ref.dtype
        )


def normalize(activations, gain):
    return pl.pallas_call(
        norm_kernel,
        out_shape=pltpu.VMEM(activations.shape, jnp.bfloat16),
        in_specs=[IN_HBM, IN_HBM],
        out_specs=IN_VMEM,
        scratch_shapes=[
            pltpu.VMEM(activations.shape, activations.dtype),
            pltpu.VMEM((gain.shape[0] // LANES, LANES), gain.dtype),
            pltpu.SemaphoreType.DMA((2,)),
        ],
        compiler_params=pltpu.CompilerParams(vmem_limit_bytes=4 * MIB),
        name="norm",
    )(far(activations), far(gain.reshape(-1, LANES)))


def swap(block, size, distance):
    return lax.ppermute(block, "mp", [(i, i ^ distance) for i in range(size)])


def after(block, *others):
    return lax.optimization_barrier((block, *others))[0]


def gather_product(me, block, size, weights, loaded, ordered):
    held = {0: block}
    distant = [d for d in (8, 12) if d < size]
    for d in distant:
        held[d] = swap(block, size, d)
    if 4 < size:
        held[4] = swap(block, size, 4)
        held[6] = swap(block, size, 6)
    held[2] = swap(block, size, 2)
    piece, token = load([weights[0]], [loaded * STEP], [0], me)
    resident = [(0, piece)]
    for d in distant:
        held[d ^ 2] = swap(after(held[d], token), size, 2)
    for d in range(0, size, 2):
        held[d ^ 1] = swap(held[d], size, 1)
    blocks = [held[r] for r in range(size)]
    depth = block.shape[1]
    return product_part(me, blocks, 0, depth, resident, weights, 0, None, True, ordered)[0]


def load_kernel(count, parts, firsts, *refs):
    sources, results, token, sems = refs[:count], refs[-count - 2 : -2], refs[-2], refs[-1]
    copies = []
    for w, (source, result, first) in enumerate(zip(sources, results, firsts)):
        rows = result.shape[0] // parts
        for i in range(parts):
            copies.append(
                pltpu.make_async_copy(
                    source.at[pl.ds(first + i * rows, rows)],
                    result.at[pl.ds(i * rows, rows)],
                    sems.at[w, i],
                )
            )
    for copy in copies:
        copy.start()
    token[0] = 0
    for copy in copies:
        copy.wait()


def load(arrays, rows, firsts, *behind):
    parts = 2
    count = len(arrays)
    shapes = [(r, *a.shape[1:]) for a, r in zip(arrays, rows)]
    size = sum(2 * math.prod(shape) for shape in shapes)
    return pl.pallas_call(
        functools.partial(load_kernel, count, parts, firsts),
        out_shape=(
            *(pltpu.VMEM(shape, a.dtype) for shape, a in zip(shapes, arrays)),
            jax.ShapeDtypeStruct((1,), jnp.int32),
        ),
        in_specs=[IN_HBM] * count + [IN_SMEM] * len(behind),
        out_specs=(IN_VMEM,) * count + (IN_SMEM,),
        scratch_shapes=[pltpu.SemaphoreType.DMA((count, parts))],
        cost_estimate=pl.CostEstimate(flops=0, bytes_accessed=int(size * 1.0), transcendentals=0),
        compiler_params=pltpu.CompilerParams(vmem_limit_bytes=MIB),
        name="load",
    )(*[far(a) for a in arrays], *behind)


def product_kernel(plan, *refs):
    count, first, depth, resident, streamed, ahead, carried, last, ordered = plan
    refs = list(refs)
    me_ref = refs.pop(0)
    blocks = [refs.pop(0) for _ in range(count)]
    held = [(at, refs.pop(0)) for at in resident]
    weights = [refs.pop(0) for _ in streamed]
    before = refs.pop(0) if carried else None
    out_ref = refs.pop(0)
    kept = refs.pop(0) if ahead else None
    if not last:
        refs.pop(0)[0] = 0
    total, sems = refs[0], refs[1]
    buffers = refs[2:]
    rows = blocks[0].shape[0]
    copies = {}
    for w, (weight, buffer, start) in enumerate(zip(weights, buffers, streamed)):
        for at in range(start, first + depth, STEP):
            copies[w, at] = pltpu.make_async_copy(
                weight.at[pl.ds(at, STEP)],
                buffer.at[pl.ds(at - start, STEP)],
                sems.at[w, (at - first) // STEP],
            )
    for key in sorted(copies, key=lambda k: (k[1], -k[0])):
        copies[key].start()
    if ahead:
        keep = pltpu.make_async_copy(
            weights[0].at[pl.ds(first + depth, ahead)], kept, sems.at[len(streamed), 0]
        )
        keep.start()

    def joined(at):
        parts = []
        for block in blocks:
            start = at if block.shape[1] >= first + depth else at - first
            parts.append(block[:, pl.ds(start, STEP)])
        return jnp.concatenate(parts, axis=0)

    for at in range(first, first + depth, STEP):
        x = joined(at)
        column = 0
        for w, (weight, buffer, start) in enumerate(zip(weights, buffers, streamed)):
            if (w, at) in copies:
                copies[w, at].wait()
                piece = buffer[pl.ds(at - start, STEP), :]
            else:
                begin, ref = [h for h in held if h[0] <= at][-1]
                piece = ref[pl.ds(at - begin, STEP), :]
            columns = pl.ds(column, weight.shape[1])
            term = jnp.dot(x, piece, preferred_element_type=jnp.float32)
            if at > first:
                total[:, columns] += term
            elif carried:
                total[:, columns] = before[:, columns] + term
            else:
                total[:, columns] = term
            column += weight.shape[1]
    if ahead:
        keep.wait()
    me = me_ref[0]
    if not last:
        out_ref[...] = total[...]
    elif ordered:
        to = lax.broadcasted_iota(jnp.int32, (count * rows, count * rows), 0)
        source = lax.broadcasted_iota(jnp.int32, (count * rows, count * rows), 1)
        place = to == ((source // rows) ^ me) * rows + source % rows
        out_ref[...] = jnp.dot(
            place.astype(jnp.bfloat16),
            total[...].astype(jnp.bfloat16),
            preferred_element_type=jnp.float32,
        ).astype(out_ref.dtype)
    else:
        for r in range(count):
            out_ref[me ^ r] = total[pl.ds(r * rows, rows), :].astype(out_ref.dtype)


def product_part(me, blocks, first, depth, resident, weights, ahead, before, last, ordered):
    count, rows = len(blocks), blocks[0].shape[0]
    columns = sum(w.shape[1] for w in weights)
    covered = first + sum(a.shape[0] for _, a in resident)
    streamed = tuple(covered if w == 0 else first for w in range(len(weights)))
    plan = (
        count, first, depth, tuple(at for at, _ in resident), streamed, ahead, before is not None, last, ordered
    )
    if not last:
        outs = [pltpu.VMEM((count * rows, columns), jnp.float32)]
        if ahead:
            outs.append(pltpu.VMEM((ahead, weights[0].shape[1]), weights[0].dtype))
        outs.append(jax.ShapeDtypeStruct((1,), jnp.int32))
    else:
        shape = (count * rows, columns) if ordered else (count, rows, columns)
        outs = [jax.ShapeDtypeStruct(shape, jnp.bfloat16)]
    spaces = [
        pltpu.VMEM((max(first + depth - start, 16), w.shape[1]), w.dtype)
        for w, start in zip(weights, streamed)
    ]
    carried = [] if before is None else [near(before)]
    return pl.pallas_call(
        functools.partial(product_kernel, plan),
        out_shape=tuple(outs),
        in_specs=[IN_SMEM]
        + [IN_VMEM] * (count + len(resident))
        + [IN_HBM] * len(weights)
        + [IN_VMEM] * len(carried),
        out_specs=tuple(IN_SMEM if o.dtype == jnp.int32 else IN_VMEM for o in outs),
        scratch_shapes=[
            pltpu.VMEM((count * rows, columns), jnp.float32),
            pltpu.SemaphoreType.DMA((len(weights) + 1, depth // STEP)),
            *spaces,
        ],
        cost_estimate=pl.CostEstimate(
            flops=2 * count * rows * depth * columns,
            bytes_accessed=depth * columns * 2,
            transcendentals=0,
        ),
        compiler_params=pltpu.CompilerParams(vmem_limit_bytes=sum(2 * a.shape[0] * a.shape[1] for a in spaces) + 6 * MIB),
        name="product",
    )(me, *[near(b) for b in blocks], *[near(a) for _, a in resident], *[far(w) for w in weights], *carried)


def attend_kernel(
    lengths_ref, query_ref, fresh_ref, cos_ref, sin_ref, key_hbm, value_hbm, out_ref, key_ref, value_ref, sems
):
    requests, heads, depth = query_ref.shape
    groups, cache = key_ref.shape[1], key_ref.shape[2]
    per_group = heads // groups
    scaling = 1.0 / math.sqrt(depth)
    copies = []
    for r in range(requests):
        copies.append(
            (
                pltpu.make_async_copy(key_hbm.at[r], key_ref.at[r], sems.at[r, 0]),
                pltpu.make_async_copy(value_hbm.at[r], value_ref.at[r], sems.at[r, 1]),
            )
        )
    for pair in copies[:2]:
        for copy in pair:
            copy.start()

    def turned(values, cosine, sine):
        widened = values.astype(jnp.float32)
        swapped = pltpu.roll(widened, depth // 2, 1)
        return (widened * cosine + swapped * sine).astype(jnp.bfloat16)

    for r in range(requests):
        cosine, sine = cos_ref[pl.ds(r, 1), :], sin_ref[pl.ds(r, 1), :]
        query = turned(query_ref[r], cosine, sine)
        fresh = fresh_ref[r]
        fresh_key = turned(fresh[:groups], cosine, sine).astype(jnp.float32)
        fresh_value = fresh[groups:].astype(jnp.float32)

        def spread(rows):
            return jnp.concatenate(
                [jnp.broadcast_to(rows[g : g + 1], (per_group, depth)) for g in range(groups)], axis=0
            )

        own = (
            jnp.sum(query.astype(jnp.float32) * spread(fresh_key), axis=1, keepdims=True) * scaling
        )
        copies[r][0].wait()
        scores = jnp.concatenate(
            [
                lax.dot_general(
                    query[g * per_group : (g + 1) * per_group],
                    key_ref[r, g],
                    (((1,), (1,)), ((), ())),
                    preferred_element_type=jnp.float32,
                )
                for g in range(groups)
            ],
            axis=0,
        )
        visible = lax.broadcasted_iota(jnp.int32, scores.shape, 1) < lengths_ref[r]
        scores = jnp.where(visible, scores * scaling, -1e30)
        highest = jnp.maximum(jnp.max(scores, axis=1, keepdims=True), own)
        weights = jnp.where(visible, jnp.exp(scores - highest), 0.0)
        own_weight = jnp.exp(own - highest)
        inverse = 1.0 / (jnp.sum(weights, axis=1, keepdims=True) + own_weight)
        probs = (weights * inverse).astype(jnp.bfloat16)
        own_prob = (own_weight * inverse).astype(jnp.bfloat16).astype(jnp.float32)
        copies[r][1].wait()
        if r + 2 < requests:
            for copy in copies[r + 2]:
                copy.start()
        mixed = jnp.concatenate(
            [
                jnp.dot(
                    probs[g * per_group : (g + 1) * per_group],
                    value_ref[r, g],
                    preferred_element_type=jnp.float32,
                )
                for g in range(groups)
            ],
            axis=0,
        )
        out_ref[r] = (mixed + own_prob * spread(fresh_value)).astype(out_ref.dtype)


def attend(arrived, query_cols, keys, values, lengths):
    size, requests, _ = arrived.shape
    depth = HEAD_DIM
    query = arrived[..., :query_cols].reshape(size, requests, -1, depth)
    query = query.transpose(1, 0, 2, 3).reshape(requests, -1, depth)
    fresh = arrived[..., query_cols:].transpose(1, 0, 2).reshape(requests, -1, depth)
    middle = depth // 2
    offsets = jnp.arange(middle, dtype=jnp.float32)
    frequency = jnp.exp(offsets * (-2.0 * math.log(rope_base) / depth))
    angles = lengths.astype(jnp.float32)[:, None] * frequency
    cosine, sine = jnp.cos(angles), jnp.sin(angles)
    attended = pl.pallas_call(
        attend_kernel,
        out_shape=jax.ShapeDtypeStruct(query.shape, jnp.bfloat16),
        in_specs=[IN_SMEM] + [IN_VMEM] * 4 + [IN_HBM] * 2,
        out_specs=IN_VMEM,
        scratch_shapes=[
            pltpu.VMEM(keys.shape, keys.dtype),
            pltpu.VMEM(values.shape, values.dtype),
            pltpu.SemaphoreType.DMA((requests, 2)),
        ],
        compiler_params=pltpu.CompilerParams(vmem_limit_bytes=14 * MIB),
        name="attend",
    )(
        lengths,
        query,
        fresh,
        jnp.concatenate([cosine, cosine], axis=1),
        jnp.concatenate([-sine, sine], axis=1),
        far(keys),
        far(values),
    )
    return attended.reshape(requests, -1)


def shards(activations, gain, q_weight, kv_weight, o_weight, key_cache, value_cache, lengths):
    size = lax.axis_size("mp")
    normed = normalize(activations, gain)
    query_cols = q_weight.shape[1]
    by_swaps = size in (4, 8, 16)
    me = lax.axis_index("mp").astype(jnp.int32).reshape(1)
    if by_swaps:
        projected = gather_product(me, normed, size, [q_weight, kv_weight], QUERY_LOADED, False)
    else:
        piece = lax.all_gather(normed, "mp", axis=0, tiled=True)
        projected = jnp.concatenate(
            [
                jnp.dot(piece, q_weight, preferred_element_type=jnp.float32),
                jnp.dot(piece, kv_weight, preferred_element_type=jnp.float32),
            ],
            axis=1,
        ).astype(jnp.bfloat16).reshape(size, normed.shape[0], -1)
    arrived = lax.all_to_all(projected, "mp", split_axis=0, concat_axis=0, tiled=True)
    attended = attend(arrived, query_cols, key_cache, value_cache, after(lengths, projected))
    if by_swaps:
        return gather_product(me, attended, size, [o_weight], OUT_LOADED, True)
    everyone = lax.all_gather(attended, "mp", axis=0, tiled=True)
    return jnp.dot(everyone, o_weight, preferred_element_type=jnp.float32).astype(jnp.bfloat16)


def solution(mesh):
    placed = (
        P(("groups", "mp"), None),
        P(),
        P(None, "mp"),
        P(None, "mp"),
        P(None, "mp"),
        P(("groups", "mp"), None, None, None),
        P(("groups", "mp"), None, None, None),
        P(("groups", "mp")),
    )
    return jax.shard_map(
        shards, mesh=mesh, in_specs=placed, out_specs=P("groups", "mp"), check_vma=False
    )
```

```python
import functools
import math

import jax
import jax.numpy as jnp
from jax import lax
from jax.experimental import pallas as pl
from jax.experimental.pallas import tpu as pltpu
from jax.sharding import PartitionSpec as P

HEADS = 128
KV_HEADS = 8
HEAD_DIM = 128
CACHE = 512

MIB = 1 << 20
STEP = 2048
LANES = 128
QUERY_LOADED = 4
OUT_LOADED = 5
PRODUCT_MIB = 30

rope_base = 500000.0
norm_eps = 1e-05

IN_VMEM = pl.BlockSpec(memory_space=pltpu.VMEM)
IN_HBM = pl.BlockSpec(memory_space=pltpu.HBM)
IN_SMEM = pl.BlockSpec(memory_space=pltpu.SMEM)


def rotate(vector, position):
    middle = vector.shape[-1] // 2
    offsets = jnp.arange(middle, dtype=jnp.float32)
    frequency = jnp.exp(offsets * (-2.0 * math.log(rope_base) / vector.shape[-1]))
    angles = position * frequency
    cosine = jnp.cos(angles)
    sine = jnp.sin(angles)
    leading = vector[..., :middle]
    trailing = vector[..., middle:]
    return jnp.concatenate(
        [leading * cosine - trailing * sine, trailing * cosine + leading * sine], axis=-1
    )


def near(array):
    return pltpu.with_memory_space_constraint(array, pltpu.VMEM)


def far(array):
    return pltpu.with_memory_space_constraint(array, pltpu.HBM)


def norm_kernel(x_hbm, gain_hbm, out_ref, x_ref, gain_ref, sems):
    copies = [
        pltpu.make_async_copy(x_hbm, x_ref, sems.at[0]),
        pltpu.make_async_copy(gain_hbm, gain_ref, sems.at[1]),
    ]
    for copy in copies:
        copy.start()
    for copy in copies:
        copy.wait()
    widened = x_ref[...].astype(jnp.float32)
    inverse = lax.rsqrt(jnp.mean(widened * widened, axis=-1, keepdims=True) + norm_eps)
    lanes = gain_ref.shape[1]
    for j in range(gain_ref.shape[0]):
        columns = pl.ds(j * lanes, lanes)
        gain = gain_ref[pl.ds(j, 1), :].astype(jnp.float32)
        out_ref[:, columns] = (x_ref[:, columns].astype(jnp.float32) * inverse * gain).astype(
            out_ref.dtype
        )


def normalize(activations, gain):
    return pl.pallas_call(
        norm_kernel,
        out_shape=pltpu.VMEM(activations.shape, jnp.bfloat16),
        in_specs=[IN_HBM, IN_HBM],
        out_specs=IN_VMEM,
        scratch_shapes=[
            pltpu.VMEM(activations.shape, activations.dtype),
            pltpu.VMEM((gain.shape[0] // LANES, LANES), gain.dtype),
            pltpu.SemaphoreType.DMA((2,)),
        ],
        compiler_params=pltpu.CompilerParams(vmem_limit_bytes=4 * MIB),
        name="norm",
    )(far(activations), far(gain.reshape(-1, LANES)))


def swap(block, size, distance):
    return lax.ppermute(block, "mp", [(i, i ^ distance) for i in range(size)])


def after(block, *others):
    return lax.optimization_barrier((block, *others))[0]


def gather_product(me, block, size, weights, loaded, ordered):
    held = {0: block}
    distant = [d for d in (8, 12) if d < size]
    for d in distant:
        held[d] = swap(block, size, d)
    if 4 < size:
        held[4] = swap(block, size, 4)
        held[6] = swap(block, size, 6)
    held[2] = swap(block, size, 2)
    piece, token = load([weights[0]], [loaded * STEP], [0], me)
    resident = [(0, piece)]
    for d in distant:
        held[d ^ 2] = swap(after(held[d], token), size, 2)
    for d in range(0, size, 2):
        held[d ^ 1] = swap(held[d], size, 1)
    blocks = [held[r] for r in range(size)]
    depth = block.shape[1]
    return product_part(me, blocks, 0, depth, resident, weights, 0, None, True, ordered)[0]


def load_kernel(count, parts, firsts, *refs):
    sources, results, token, sems = refs[:count], refs[-count - 2 : -2], refs[-2], refs[-1]
    copies = []
    for w, (source, result, first) in enumerate(zip(sources, results, firsts)):
        rows = result.shape[0] // parts
        for i in range(parts):
            copies.append(
                pltpu.make_async_copy(
                    source.at[pl.ds(first + i * rows, rows)],
                    result.at[pl.ds(i * rows, rows)],
                    sems.at[w, i],
                )
            )
    for copy in copies:
        copy.start()
    token[0] = 0
    for copy in copies:
        copy.wait()


def load(arrays, rows, firsts, *behind):
    parts = 2 if all(r % 2 == 0 for r in rows) else 1
    count = len(arrays)
    shapes = [(r, *a.shape[1:]) for a, r in zip(arrays, rows)]
    size = sum(2 * math.prod(shape) for shape in shapes)
    return pl.pallas_call(
        functools.partial(load_kernel, count, parts, firsts),
        out_shape=(
            *(pltpu.VMEM(shape, a.dtype) for shape, a in zip(shapes, arrays)),
            jax.ShapeDtypeStruct((1,), jnp.int32),
        ),
        in_specs=[IN_HBM] * count + [pl.BlockSpec(memory_space=pl.ANY)] * len(behind),
        out_specs=(IN_VMEM,) * count + (IN_SMEM,),
        scratch_shapes=[pltpu.SemaphoreType.DMA((count, parts))],
        cost_estimate=pl.CostEstimate(flops=0, bytes_accessed=int(size * 1.0), transcendentals=0),
        compiler_params=pltpu.CompilerParams(vmem_limit_bytes=MIB),
        name="load",
    )(*[far(a) for a in arrays], *behind)


def product_kernel(plan, *refs):
    count, first, depth, resident, streamed, ahead, carried, last, ordered = plan
    refs = list(refs)
    me_ref = refs.pop(0)
    blocks = [refs.pop(0) for _ in range(count)]
    held = [(at, refs.pop(0)) for at in resident]
    weights = [refs.pop(0) for _ in streamed]
    before = refs.pop(0) if carried else None
    out_ref = refs.pop(0)
    kept = refs.pop(0) if ahead else None
    if not last:
        refs.pop(0)[0] = 0
    total, sems = refs[0], refs[1]
    buffers = refs[2:]
    rows = blocks[0].shape[0]
    copies = {}
    for w, (weight, buffer, start) in enumerate(zip(weights, buffers, streamed)):
        for at in range(start, first + depth, STEP):
            copies[w, at] = pltpu.make_async_copy(
                weight.at[pl.ds(at, STEP)],
                buffer.at[pl.ds(at - start, STEP)],
                sems.at[w, (at - first) // STEP],
            )
    for key in sorted(copies, key=lambda k: (k[1], -k[0])):
        copies[key].start()
    if ahead:
        keep = pltpu.make_async_copy(
            weights[0].at[pl.ds(first + depth, ahead)], kept, sems.at[len(streamed), 0]
        )
        keep.start()

    def joined(at):
        parts = []
        for block in blocks:
            start = at if block.shape[1] >= first + depth else at - first
            parts.append(block[:, pl.ds(start, STEP)])
        return jnp.concatenate(parts, axis=0)

    for at in range(first, first + depth, STEP):
        x = joined(at)
        column = 0
        for w, (weight, buffer, start) in enumerate(zip(weights, buffers, streamed)):
            if (w, at) in copies:
                copies[w, at].wait()
                piece = buffer[pl.ds(at - start, STEP), :]
            else:
                begin, ref = [h for h in held if h[0] <= at][-1]
                piece = ref[pl.ds(at - begin, STEP), :]
            columns = pl.ds(column, weight.shape[1])
            term = jnp.dot(x, piece, preferred_element_type=jnp.float32)
            if at > first:
                total[:, columns] += term
            elif carried:
                total[:, columns] = before[:, columns] + term
            else:
                total[:, columns] = term
            column += weight.shape[1]
    if ahead:
        keep.wait()
    me = me_ref[0]
    if not last:
        out_ref[...] = total[...]
    elif ordered:
        to = lax.broadcasted_iota(jnp.int32, (count * rows, count * rows), 0)
        source = lax.broadcasted_iota(jnp.int32, (count * rows, count * rows), 1)
        place = to == ((source // rows) ^ me) * rows + source % rows
        out_ref[...] = jnp.dot(
            place.astype(jnp.bfloat16),
            total[...].astype(jnp.bfloat16),
            preferred_element_type=jnp.float32,
        ).astype(out_ref.dtype)
    else:
        for r in range(count):
            out_ref[me ^ r] = total[pl.ds(r * rows, rows), :].astype(out_ref.dtype)


def product_part(me, blocks, first, depth, resident, weights, ahead, before, last, ordered):
    count, rows = len(blocks), blocks[0].shape[0]
    columns = sum(w.shape[1] for w in weights)
    covered = first + sum(a.shape[0] for _, a in resident)
    streamed = tuple(covered if w == 0 else first for w in range(len(weights)))
    plan = (
        count, first, depth, tuple(at for at, _ in resident), streamed, ahead, before is not None, last, ordered
    )
    if not last:
        outs = [pltpu.VMEM((count * rows, columns), jnp.float32)]
        if ahead:
            outs.append(pltpu.VMEM((ahead, weights[0].shape[1]), weights[0].dtype))
        outs.append(jax.ShapeDtypeStruct((1,), jnp.int32))
    else:
        shape = (count * rows, columns) if ordered else (count, rows, columns)
        outs = [jax.ShapeDtypeStruct(shape, jnp.bfloat16)]
    spaces = [
        pltpu.VMEM((max(first + depth - start, 16), w.shape[1]), w.dtype)
        for w, start in zip(weights, streamed)
    ]
    carried = [] if before is None else [near(before)]
    return pl.pallas_call(
        functools.partial(product_kernel, plan),
        out_shape=tuple(outs),
        in_specs=[IN_SMEM]
        + [IN_VMEM] * (count + len(resident))
        + [IN_HBM] * len(weights)
        + [IN_VMEM] * len(carried),
        out_specs=tuple(IN_SMEM if o.dtype == jnp.int32 else IN_VMEM for o in outs),
        scratch_shapes=[
            pltpu.VMEM((count * rows, columns), jnp.float32),
            pltpu.SemaphoreType.DMA((len(weights) + 1, depth // STEP)),
            *spaces,
        ],
        cost_estimate=pl.CostEstimate(
            flops=2 * count * rows * depth * columns,
            bytes_accessed=depth * columns * 2,
            transcendentals=0,
        ),
        compiler_params=pltpu.CompilerParams(vmem_limit_bytes=sum(2 * a.shape[0] * a.shape[1] for a in spaces) + 6 * MIB),
        name="product",
    )(me, *[near(b) for b in blocks], *[near(a) for _, a in resident], *[far(w) for w in weights], *carried)


def attend_kernel(
    lengths_ref,
    query_ref,
    fresh_ref,
    cos_ref,
    sin_ref,
    first_key_ref,
    first_value_ref,
    key_hbm,
    value_hbm,
    out_ref,
    key_ref,
    value_ref,
    sems,
):
    requests, heads, depth = query_ref.shape
    groups = key_ref.shape[1]
    per_group = heads // groups
    scaling = 1.0 / math.sqrt(depth)
    copies = []
    for r in range(1, requests):
        copies.append(
            (
                pltpu.make_async_copy(key_hbm.at[r], key_ref.at[r - 1], sems.at[r - 1, 0]),
                pltpu.make_async_copy(value_hbm.at[r], value_ref.at[r - 1], sems.at[r - 1, 1]),
            )
        )
    for pair in copies:
        for copy in pair:
            copy.start()

    def turned(values, cosine, sine):
        widened = values.astype(jnp.float32)
        swapped = pltpu.roll(widened, depth // 2, 1)
        return (widened * cosine + swapped * sine).astype(jnp.bfloat16)

    for r in range(requests):
        cosine, sine = cos_ref[pl.ds(r, 1), :], sin_ref[pl.ds(r, 1), :]
        query = turned(query_ref[r], cosine, sine)
        fresh = fresh_ref[r]
        fresh_key = turned(fresh[:groups], cosine, sine).astype(jnp.float32)
        fresh_value = fresh[groups:].astype(jnp.float32)

        def spread(rows):
            return jnp.concatenate(
                [jnp.broadcast_to(rows[g : g + 1], (per_group, depth)) for g in range(groups)], axis=0
            )

        own = (
            jnp.sum(query.astype(jnp.float32) * spread(fresh_key), axis=1, keepdims=True) * scaling
        )
        if r > 0:
            copies[r - 1][0].wait()
            keys = key_ref.at[r - 1]
        else:
            keys = first_key_ref.at[0]
        scores = jnp.concatenate(
            [
                lax.dot_general(
                    query[g * per_group : (g + 1) * per_group],
                    keys[g],
                    (((1,), (1,)), ((), ())),
                    preferred_element_type=jnp.float32,
                )
                for g in range(groups)
            ],
            axis=0,
        )
        visible = lax.broadcasted_iota(jnp.int32, scores.shape, 1) < lengths_ref[r]
        scores = jnp.where(visible, scores * scaling, -1e30)
        highest = jnp.maximum(jnp.max(scores, axis=1, keepdims=True), own)
        weights = jnp.where(visible, jnp.exp(scores - highest), 0.0)
        own_weight = jnp.exp(own - highest)
        inverse = 1.0 / (jnp.sum(weights, axis=1, keepdims=True) + own_weight)
        probs = (weights * inverse).astype(jnp.bfloat16)
        own_prob = (own_weight * inverse).astype(jnp.bfloat16).astype(jnp.float32)
        if r > 0:
            copies[r - 1][1].wait()
            values = value_ref.at[r - 1]
        else:
            values = first_value_ref.at[0]
        mixed = jnp.concatenate(
            [
                jnp.dot(
                    probs[g * per_group : (g + 1) * per_group],
                    values[g],
                    preferred_element_type=jnp.float32,
                )
                for g in range(groups)
            ],
            axis=0,
        )
        out_ref[r] = (mixed + own_prob * spread(fresh_value)).astype(out_ref.dtype)


def attend(arrived, query_cols, keys, values, first_key, first_value, lengths):
    size, requests, _ = arrived.shape
    depth = HEAD_DIM
    query = arrived[..., :query_cols].reshape(size, requests, -1, depth)
    query = query.transpose(1, 0, 2, 3).reshape(requests, -1, depth)
    fresh = arrived[..., query_cols:].transpose(1, 0, 2).reshape(requests, -1, depth)
    middle = depth // 2
    offsets = jnp.arange(middle, dtype=jnp.float32)
    frequency = jnp.exp(offsets * (-2.0 * math.log(rope_base) / depth))
    angles = lengths.astype(jnp.float32)[:, None] * frequency
    cosine, sine = jnp.cos(angles), jnp.sin(angles)
    attended = pl.pallas_call(
        attend_kernel,
        out_shape=jax.ShapeDtypeStruct(query.shape, jnp.bfloat16),
        in_specs=[IN_SMEM] + [IN_VMEM] * 6 + [IN_HBM] * 2,
        out_specs=IN_VMEM,
        scratch_shapes=[
            pltpu.VMEM((requests - 1, *keys.shape[1:]), keys.dtype),
            pltpu.VMEM((requests - 1, *values.shape[1:]), values.dtype),
            pltpu.SemaphoreType.DMA((requests - 1, 2)),
        ],
        compiler_params=pltpu.CompilerParams(vmem_limit_bytes=14 * MIB),
        name="attend",
    )(
        lengths,
        query,
        fresh,
        jnp.concatenate([cosine, cosine], axis=1),
        jnp.concatenate([-sine, sine], axis=1),
        near(first_key),
        near(first_value),
        far(keys),
        far(values),
    )
    return attended.reshape(requests, -1)


def shards(activations, gain, q_weight, kv_weight, o_weight, key_cache, value_cache, lengths):
    size = lax.axis_size("mp")
    normed = normalize(activations, gain)
    query_cols = q_weight.shape[1]
    by_swaps = size in (4, 8, 16)
    me = lax.axis_index("mp").astype(jnp.int32).reshape(1)
    if by_swaps:
        projected = gather_product(me, normed, size, [q_weight, kv_weight], QUERY_LOADED, False)
    else:
        piece = lax.all_gather(normed, "mp", axis=0, tiled=True)
        projected = jnp.concatenate(
            [
                jnp.dot(piece, q_weight, preferred_element_type=jnp.float32),
                jnp.dot(piece, kv_weight, preferred_element_type=jnp.float32),
            ],
            axis=1,
        ).astype(jnp.bfloat16).reshape(size, normed.shape[0], -1)
    arrived = lax.all_to_all(projected, "mp", split_axis=0, concat_axis=0, tiled=True)
    first_key, first_value, _ = load([key_cache, value_cache], [1, 1], [0, 0], projected)
    attended = attend(
        arrived, query_cols, key_cache, value_cache, first_key, first_value, after(lengths, projected)
    )
    if by_swaps:
        return gather_product(me, attended, size, [o_weight], OUT_LOADED, True)
    everyone = lax.all_gather(attended, "mp", axis=0, tiled=True)
    return jnp.dot(everyone, o_weight, preferred_element_type=jnp.float32).astype(jnp.bfloat16)


def solution(mesh):
    placed = (
        P(("groups", "mp"), None),
        P(),
        P(None, "mp"),
        P(None, "mp"),
        P(None, "mp"),
        P(("groups", "mp"), None, None, None),
        P(("groups", "mp"), None, None, None),
        P(("groups", "mp")),
    )
    return jax.shard_map(
        shards, mesh=mesh, in_specs=placed, out_specs=P("groups", "mp"), check_vma=False
    )
```

```python
import functools
import math

import jax
import jax.numpy as jnp
from jax import lax
from jax.experimental import pallas as pl
from jax.experimental.pallas import tpu as pltpu
from jax.sharding import PartitionSpec as P

HEADS = 128
KV_HEADS = 8
HEAD_DIM = 128
CACHE = 512

MIB = 1 << 20
STEP = 2048
LANES = 128
QUERY_LOADED = 4
OUT_LOADED = 5
PRODUCT_MIB = 30

rope_base = 500000.0
norm_eps = 1e-05

IN_VMEM = pl.BlockSpec(memory_space=pltpu.VMEM)
IN_HBM = pl.BlockSpec(memory_space=pltpu.HBM)
IN_SMEM = pl.BlockSpec(memory_space=pltpu.SMEM)


def rotate(vector, position):
    middle = vector.shape[-1] // 2
    offsets = jnp.arange(middle, dtype=jnp.float32)
    frequency = jnp.exp(offsets * (-2.0 * math.log(rope_base) / vector.shape[-1]))
    angles = position * frequency
    cosine = jnp.cos(angles)
    sine = jnp.sin(angles)
    leading = vector[..., :middle]
    trailing = vector[..., middle:]
    return jnp.concatenate(
        [leading * cosine - trailing * sine, trailing * cosine + leading * sine], axis=-1
    )


def near(array):
    return pltpu.with_memory_space_constraint(array, pltpu.VMEM)


def far(array):
    return pltpu.with_memory_space_constraint(array, pltpu.HBM)


def norm_kernel(x_hbm, gain_hbm, out_ref, x_ref, gain_ref, sems):
    copies = [
        pltpu.make_async_copy(x_hbm, x_ref, sems.at[0]),
        pltpu.make_async_copy(gain_hbm, gain_ref, sems.at[1]),
    ]
    for copy in copies:
        copy.start()
    for copy in copies:
        copy.wait()
    widened = x_ref[...].astype(jnp.float32)
    inverse = lax.rsqrt(jnp.mean(widened * widened, axis=-1, keepdims=True) + norm_eps)
    lanes = gain_ref.shape[1]
    for j in range(gain_ref.shape[0]):
        columns = pl.ds(j * lanes, lanes)
        gain = gain_ref[pl.ds(j, 1), :].astype(jnp.float32)
        out_ref[:, columns] = (x_ref[:, columns].astype(jnp.float32) * inverse * gain).astype(
            out_ref.dtype
        )


def normalize(activations, gain):
    return pl.pallas_call(
        norm_kernel,
        out_shape=pltpu.VMEM(activations.shape, jnp.bfloat16),
        in_specs=[IN_HBM, IN_HBM],
        out_specs=IN_VMEM,
        scratch_shapes=[
            pltpu.VMEM(activations.shape, activations.dtype),
            pltpu.VMEM((gain.shape[0] // LANES, LANES), gain.dtype),
            pltpu.SemaphoreType.DMA((2,)),
        ],
        compiler_params=pltpu.CompilerParams(vmem_limit_bytes=4 * MIB),
        name="norm",
    )(far(activations), far(gain.reshape(-1, LANES)))


def swap(block, size, distance):
    return lax.ppermute(block, "mp", [(i, i ^ distance) for i in range(size)])


def after(block, *others):
    return lax.optimization_barrier((block, *others))[0]


def gather_product(me, block, size, weights, loaded, ordered):
    held = {0: block}
    distant = [d for d in (8, 12) if d < size]
    for d in distant:
        held[d] = swap(block, size, d)
    held[2] = swap(block, size, 2)
    if 4 < size:
        held[4] = swap(block, size, 4)
        held[6] = swap(held[2], size, 4)
    piece, token = load([weights[0]], [loaded * STEP], [0], me)
    resident = [(0, piece)]
    for d in distant:
        held[d ^ 2] = swap(after(held[d], token), size, 2)
    for d in range(0, size, 2):
        held[d ^ 1] = swap(held[d], size, 1)
    blocks = [held[r] for r in range(size)]
    depth = block.shape[1]
    return product_part(me, blocks, 0, depth, resident, weights, 0, None, True, ordered)[0]


def load_kernel(count, parts, firsts, *refs):
    sources, results, token, sems = refs[:count], refs[-count - 2 : -2], refs[-2], refs[-1]
    copies = []
    for w, (source, result, first) in enumerate(zip(sources, results, firsts)):
        rows = result.shape[0] // parts
        for i in range(parts):
            copies.append(
                pltpu.make_async_copy(
                    source.at[pl.ds(first + i * rows, rows)],
                    result.at[pl.ds(i * rows, rows)],
                    sems.at[w, i],
                )
            )
    for copy in copies:
        copy.start()
    token[0] = 0
    for copy in copies:
        copy.wait()


def load(arrays, rows, firsts, *behind):
    parts = 2 if all(r % 2 == 0 for r in rows) else 1
    count = len(arrays)
    shapes = [(r, *a.shape[1:]) for a, r in zip(arrays, rows)]
    size = sum(2 * math.prod(shape) for shape in shapes)
    return pl.pallas_call(
        functools.partial(load_kernel, count, parts, firsts),
        out_shape=(
            *(pltpu.VMEM(shape, a.dtype) for shape, a in zip(shapes, arrays)),
            jax.ShapeDtypeStruct((1,), jnp.int32),
        ),
        in_specs=[IN_HBM] * count + [pl.BlockSpec(memory_space=pl.ANY)] * len(behind),
        out_specs=(IN_VMEM,) * count + (IN_SMEM,),
        scratch_shapes=[pltpu.SemaphoreType.DMA((count, parts))],
        cost_estimate=pl.CostEstimate(flops=0, bytes_accessed=25165824, transcendentals=0),
        compiler_params=pltpu.CompilerParams(vmem_limit_bytes=MIB),
        name="load",
    )(*[far(a) for a in arrays], *behind)


def product_kernel(plan, *refs):
    count, first, depth, resident, streamed, ahead, carried, last, ordered = plan
    refs = list(refs)
    me_ref = refs.pop(0)
    blocks = [refs.pop(0) for _ in range(count)]
    held = [(at, refs.pop(0)) for at in resident]
    weights = [refs.pop(0) for _ in streamed]
    before = refs.pop(0) if carried else None
    out_ref = refs.pop(0)
    kept = refs.pop(0) if ahead else None
    if not last:
        refs.pop(0)[0] = 0
    total, sems = refs[0], refs[1]
    buffers = refs[2:]
    rows = blocks[0].shape[0]
    copies = {}
    for w, (weight, buffer, start) in enumerate(zip(weights, buffers, streamed)):
        for at in range(start, first + depth, STEP):
            copies[w, at] = pltpu.make_async_copy(
                weight.at[pl.ds(at, STEP)],
                buffer.at[pl.ds(at - start, STEP)],
                sems.at[w, (at - first) // STEP],
            )
    for key in sorted(copies, key=lambda k: (k[1], -k[0])):
        copies[key].start()
    if ahead:
        keep = pltpu.make_async_copy(
            weights[0].at[pl.ds(first + depth, ahead)], kept, sems.at[len(streamed), 0]
        )
        keep.start()

    def joined(at):
        parts = []
        for block in blocks:
            start = at if block.shape[1] >= first + depth else at - first
            parts.append(block[:, pl.ds(start, STEP)])
        return jnp.concatenate(parts, axis=0)

    for at in range(first, first + depth, STEP):
        x = joined(at)
        column = 0
        for w, (weight, buffer, start) in enumerate(zip(weights, buffers, streamed)):
            if (w, at) in copies:
                copies[w, at].wait()
                piece = buffer[pl.ds(at - start, STEP), :]
            else:
                begin, ref = [h for h in held if h[0] <= at][-1]
                piece = ref[pl.ds(at - begin, STEP), :]
            columns = pl.ds(column, weight.shape[1])
            term = jnp.dot(x, piece, preferred_element_type=jnp.float32)
            if at > first:
                total[:, columns] += term
            elif carried:
                total[:, columns] = before[:, columns] + term
            else:
                total[:, columns] = term
            column += weight.shape[1]
    if ahead:
        keep.wait()
    me = me_ref[0]
    if not last:
        out_ref[...] = total[...]
    elif ordered:
        to = lax.broadcasted_iota(jnp.int32, (count * rows, count * rows), 0)
        source = lax.broadcasted_iota(jnp.int32, (count * rows, count * rows), 1)
        place = to == ((source // rows) ^ me) * rows + source % rows
        out_ref[...] = jnp.dot(
            place.astype(jnp.bfloat16),
            total[...].astype(jnp.bfloat16),
            preferred_element_type=jnp.float32,
        ).astype(out_ref.dtype)
    else:
        for r in range(count):
            out_ref[me ^ r] = total[pl.ds(r * rows, rows), :].astype(out_ref.dtype)


def product_part(me, blocks, first, depth, resident, weights, ahead, before, last, ordered):
    count, rows = len(blocks), blocks[0].shape[0]
    columns = sum(w.shape[1] for w in weights)
    covered = first + sum(a.shape[0] for _, a in resident)
    streamed = tuple(covered if w == 0 else first for w in range(len(weights)))
    plan = (
        count, first, depth, tuple(at for at, _ in resident), streamed, ahead, before is not None, last, ordered
    )
    if not last:
        outs = [pltpu.VMEM((count * rows, columns), jnp.float32)]
        if ahead:
            outs.append(pltpu.VMEM((ahead, weights[0].shape[1]), weights[0].dtype))
        outs.append(jax.ShapeDtypeStruct((1,), jnp.int32))
    else:
        shape = (count * rows, columns) if ordered else (count, rows, columns)
        outs = [jax.ShapeDtypeStruct(shape, jnp.bfloat16)]
    spaces = [
        pltpu.VMEM((max(first + depth - start, 16), w.shape[1]), w.dtype)
        for w, start in zip(weights, streamed)
    ]
    carried = [] if before is None else [near(before)]
    return pl.pallas_call(
        functools.partial(product_kernel, plan),
        out_shape=tuple(outs),
        in_specs=[IN_SMEM]
        + [IN_VMEM] * (count + len(resident))
        + [IN_HBM] * len(weights)
        + [IN_VMEM] * len(carried),
        out_specs=tuple(IN_SMEM if o.dtype == jnp.int32 else IN_VMEM for o in outs),
        scratch_shapes=[
            pltpu.VMEM((count * rows, columns), jnp.float32),
            pltpu.SemaphoreType.DMA((len(weights) + 1, depth // STEP)),
            *spaces,
        ],
        cost_estimate=pl.CostEstimate(
            flops=2 * count * rows * depth * columns,
            bytes_accessed=depth * columns * 2,
            transcendentals=0,
        ),
        compiler_params=pltpu.CompilerParams(vmem_limit_bytes=sum(2 * a.shape[0] * a.shape[1] for a in spaces) + 6 * MIB),
        name="product",
    )(me, *[near(b) for b in blocks], *[near(a) for _, a in resident], *[far(w) for w in weights], *carried)


def attend_kernel(
    lengths_ref,
    query_ref,
    fresh_ref,
    cos_ref,
    sin_ref,
    first_key_ref,
    first_value_ref,
    key_hbm,
    value_hbm,
    out_ref,
    key_ref,
    value_ref,
    sems,
):
    requests, heads, depth = query_ref.shape
    groups = key_ref.shape[1]
    per_group = heads // groups
    scaling = 1.0 / math.sqrt(depth)
    copies = []
    for r in range(1, requests):
        copies.append(
            (
                pltpu.make_async_copy(key_hbm.at[r], key_ref.at[r - 1], sems.at[r - 1, 0]),
                pltpu.make_async_copy(value_hbm.at[r], value_ref.at[r - 1], sems.at[r - 1, 1]),
            )
        )
    for pair in copies:
        for copy in pair:
            copy.start()

    def turned(values, cosine, sine):
        widened = values.astype(jnp.float32)
        swapped = pltpu.roll(widened, depth // 2, 1)
        return (widened * cosine + swapped * sine).astype(jnp.bfloat16)

    for r in range(requests):
        cosine, sine = cos_ref[pl.ds(r, 1), :], sin_ref[pl.ds(r, 1), :]
        query = turned(query_ref[r], cosine, sine)
        fresh = fresh_ref[r]
        fresh_key = turned(fresh[:groups], cosine, sine).astype(jnp.float32)
        fresh_value = fresh[groups:].astype(jnp.float32)

        def spread(rows):
            return jnp.concatenate(
                [jnp.broadcast_to(rows[g : g + 1], (per_group, depth)) for g in range(groups)], axis=0
            )

        own = (
            jnp.sum(query.astype(jnp.float32) * spread(fresh_key), axis=1, keepdims=True) * scaling
        )
        if r > 0:
            copies[r - 1][0].wait()
            keys = key_ref.at[r - 1]
        else:
            keys = first_key_ref.at[0]
        scores = jnp.concatenate(
            [
                lax.dot_general(
                    query[g * per_group : (g + 1) * per_group],
                    keys[g],
                    (((1,), (1,)), ((), ())),
                    preferred_element_type=jnp.float32,
                )
                for g in range(groups)
            ],
            axis=0,
        )
        visible = lax.broadcasted_iota(jnp.int32, scores.shape, 1) < lengths_ref[r]
        scores = jnp.where(visible, scores * scaling, -1e30)
        highest = jnp.maximum(jnp.max(scores, axis=1, keepdims=True), own)
        weights = jnp.where(visible, jnp.exp(scores - highest), 0.0)
        own_weight = jnp.exp(own - highest)
        inverse = 1.0 / (jnp.sum(weights, axis=1, keepdims=True) + own_weight)
        probs = (weights * inverse).astype(jnp.bfloat16)
        own_prob = (own_weight * inverse).astype(jnp.bfloat16).astype(jnp.float32)
        if r > 0:
            copies[r - 1][1].wait()
            values = value_ref.at[r - 1]
        else:
            values = first_value_ref.at[0]
        mixed = jnp.concatenate(
            [
                jnp.dot(
                    probs[g * per_group : (g + 1) * per_group],
                    values[g],
                    preferred_element_type=jnp.float32,
                )
                for g in range(groups)
            ],
            axis=0,
        )
        out_ref[r] = (mixed + own_prob * spread(fresh_value)).astype(out_ref.dtype)


def attend(arrived, query_cols, keys, values, first_key, first_value, lengths):
    size, requests, _ = arrived.shape
    depth = HEAD_DIM
    query = arrived[..., :query_cols].reshape(size, requests, -1, depth)
    query = query.transpose(1, 0, 2, 3).reshape(requests, -1, depth)
    fresh = arrived[..., query_cols:].transpose(1, 0, 2).reshape(requests, -1, depth)
    middle = depth // 2
    offsets = jnp.arange(middle, dtype=jnp.float32)
    frequency = jnp.exp(offsets * (-2.0 * math.log(rope_base) / depth))
    angles = lengths.astype(jnp.float32)[:, None] * frequency
    cosine, sine = jnp.cos(angles), jnp.sin(angles)
    attended = pl.pallas_call(
        attend_kernel,
        out_shape=jax.ShapeDtypeStruct(query.shape, jnp.bfloat16),
        in_specs=[IN_SMEM] + [IN_VMEM] * 6 + [IN_HBM] * 2,
        out_specs=IN_VMEM,
        scratch_shapes=[
            pltpu.VMEM((requests - 1, *keys.shape[1:]), keys.dtype),
            pltpu.VMEM((requests - 1, *values.shape[1:]), values.dtype),
            pltpu.SemaphoreType.DMA((requests - 1, 2)),
        ],
        compiler_params=pltpu.CompilerParams(vmem_limit_bytes=14 * MIB),
        name="attend",
    )(
        lengths,
        query,
        fresh,
        jnp.concatenate([cosine, cosine], axis=1),
        jnp.concatenate([-sine, sine], axis=1),
        near(first_key),
        near(first_value),
        far(keys),
        far(values),
    )
    return attended.reshape(requests, -1)


def shards(activations, gain, q_weight, kv_weight, o_weight, key_cache, value_cache, lengths):
    size = lax.axis_size("mp")
    normed = normalize(activations, gain)
    query_cols = q_weight.shape[1]
    by_swaps = size in (4, 8, 16)
    me = lax.axis_index("mp").astype(jnp.int32).reshape(1)
    if by_swaps:
        projected = gather_product(me, normed, size, [q_weight, kv_weight], QUERY_LOADED, False)
    else:
        piece = lax.all_gather(normed, "mp", axis=0, tiled=True)
        projected = jnp.concatenate(
            [
                jnp.dot(piece, q_weight, preferred_element_type=jnp.float32),
                jnp.dot(piece, kv_weight, preferred_element_type=jnp.float32),
            ],
            axis=1,
        ).astype(jnp.bfloat16).reshape(size, normed.shape[0], -1)
    arrived = lax.all_to_all(projected, "mp", split_axis=0, concat_axis=0, tiled=True)
    first_key, first_value, _ = load([key_cache, value_cache], [1, 1], [0, 0], projected)
    attended = attend(
        arrived, query_cols, key_cache, value_cache, first_key, first_value, after(lengths, projected)
    )
    if by_swaps:
        return gather_product(me, attended, size, [o_weight], OUT_LOADED, True)
    everyone = lax.all_gather(attended, "mp", axis=0, tiled=True)
    return jnp.dot(everyone, o_weight, preferred_element_type=jnp.float32).astype(jnp.bfloat16)


def solution(mesh):
    placed = (
        P(("groups", "mp"), None),
        P(),
        P(None, "mp"),
        P(None, "mp"),
        P(None, "mp"),
        P(("groups", "mp"), None, None, None),
        P(("groups", "mp"), None, None, None),
        P(("groups", "mp")),
    )
    return jax.shard_map(
        shards, mesh=mesh, in_specs=placed, out_specs=P("groups", "mp"), check_vma=False
    )
```
